32 devices in a mesh: grp: 2 (over y), row: 4 (over z), det: 2 (over x), sub: 2 (over core).
Axes of the slice: x: 2, y: 2, z: 4, core: 2. Of those that a mesh axis runs over, the one named last changes fastest.
Arguments:
- patterns: float32 [8, 4096, 512], P(('grp', 'row'), ('det', 'sub')), parts along dimension 0, may hold values from -6 to 6
- jitter: int32 [8], P(('grp', 'row')), parts along dimension 0, may hold values from -8 to 8
- subpixel: int32 [8], P(('grp', 'row')), parts along dimension 0, may hold values from 0 to 15
- kernels: float32 [16, 4], replicated, may hold values from -3 to 3
- intersection: int32 [4, 4, 4], P(('det', 'sub'), None, 'row'), may hold values 0 or 1
- owners: int32 [4, 4, 1], P(('det', 'sub')), may hold values from 0 to 3; in each aligned block of 4 rows (0 to 3, 4 to 7, ..., all dimensions but the last counted through in order) at most 2 rows name the same one
- wigner: float32 [2, 64, 64], replicated, may hold values from -6 to 6
Outputs:
- object_slots: float32 [8, 4, 2, 64, 256], P(('grp', 'det', 'sub'), 'row'), parts along dimension 0
The draws below stay inside these ranges and needn't reach their ends.
There are 2 independent parts, one for each index of `grp`. The reference program is written for one: setup_inputs(seed, part) draws one part's arguments, and reference() takes and returns one part's arrays. A program takes and returns all parts, laid end to end along the dimension named above; an argument that names none is the same for every part. Nothing has to cross between parts.
Inputs may be any that keep to these rules, and one draw needn't show every extreme that they name: For each s, no owner appears more than 2 times among owners[s, :, 0]; some owner appears exactly 2 times in some s.
All inputs are finite; a program needn't handle non-finite values. No bound on the sum of `intersection` on one device may be relied on, other than what follows from the above.
Results may differ from the reference program's by a relative error of at most 0.0003.
Values sent between devices are 32-bit elements; how exact they have to be, the bound alone decides.
A program may use at most 128 MiB of HBM per device.

```python
import math
import jax
import jax.numpy as jnp
import numpy as np
from jax import lax

KY = 64
KX = 64
SX = 512
TAPS = 4
NPHASE = 16
KD = 4096
SY = 4
DS = 4
SXS = 128
PB = 1024
CAP = 2
N_ROW = 4


def with_ends(array, rng, low, top_value):
    spot = [jax.random.randint(jax.random.fold_in(rng, axis), (), 0, length) for axis, length in enumerate(array.shape)]
    widest = array.shape.index(max(array.shape))
    next_to = spot[:widest] + [(spot[widest] + 1) % array.shape[widest]] + spot[widest + 1:]
    return array.at[tuple(spot)].set(low).at[tuple(next_to)].set(top_value)


def level_of(stream_key, dims, cuts, smallest, high):
    loudness, own = 1.0, jax.random.fold_in(stream_key, 6)
    for axis_at, shards_of in cuts:
        steps = jnp.exp(jax.random.uniform(jax.random.fold_in(own, axis_at), (shards_of,), jnp.float32, smallest / len(cuts), high / len(cuts)))
        loudness = loudness * jnp.repeat(steps, dims[axis_at] // shards_of).reshape([-1 if axis == axis_at else 1 for axis in range(len(dims))])
    return loudness


def routed_block(own_key, own, number, rows, amount, top, reach, slope):
    order = jax.random.permutation(own_key, amount)
    heavy_load, usual = load_shares(amount, rows * top, reach, slope, True), load_shares(amount, rows * top, reach, slope, False)
    places = jnp.arange(amount)

    def named(sizes, turn):
        used = int((sizes > 0).sum())
        fixed = max(1, used // 4)
        moved = fixed + (places - fixed + turn * (used - fixed)) % max(1, amount - fixed)
        return jnp.zeros((amount,), jnp.int32).at[order[jnp.where(places < fixed, places, moved)]].set(jnp.asarray(sizes, jnp.int32))

    sizes = jnp.where(number % 4 == 0, named(heavy_load, number // 4), named(usual, number - number // 4 - 1))
    mixed = jax.random.permutation(jax.random.fold_in(own, 3), amount)
    source_of, sink = mixed[0:amount // 2 * 2:2], mixed[1:amount // 2 * 2:2]
    slack = jnp.minimum(sizes[source_of] - 1, reach - sizes[sink]) // 2
    slack = jnp.where((source_of == order[0]) | (sink == order[0]) | (sizes[sink] == 0), 0, jnp.maximum(slack, 0))
    moved = jax.random.randint(jax.random.fold_in(own, 4), (amount // 2,), 0, 1 << 20) % (slack + 1)
    sizes = sizes.at[source_of].add(-moved).at[sink].add(moved)
    members = jnp.searchsorted(jnp.cumsum(sizes), jnp.arange(rows * top), side="right").astype(jnp.int32)
    grid = members.reshape(top, rows).T
    grid = grid[jax.random.permutation(jax.random.fold_in(own, 1), rows)]
    turn = jax.random.randint(jax.random.fold_in(own, 2), (rows, 1), 0, top)
    return jnp.take_along_axis(grid, (jnp.arange(top)[None, :] + turn) % top, axis=1)


def load_shares(number_of, total, bound, lean, full):
    portions = [(1 << 20) // math.isqrt(standing ** lean) + 1 for standing in range(1, number_of + 1)]
    largest = bound if full else min(bound, max(-(-total // number_of), total * portions[0] // sum(portions)))
    least = 1 if total - largest >= number_of - 1 else 0
    holding, spare = [largest] + [least] * (number_of - 1), total - largest - least * (number_of - 1)
    while spare > 0:
        movable = [i for i in range(1, number_of) if holding[i] < largest] or [i for i in range(1, number_of) if holding[i] < bound]
        mass, budget = sum([portions[i] for i in movable]), spare
        for i in movable:
            more = min(bound - holding[i], max(1, budget * portions[i] // mass), spare)
            holding[i] = holding[i] + more
            spare = spare - more
    return np.array(holding)


def noise(own_key, dims, spread, limit, cuts=(), kind=jnp.bfloat16):
    result = spread * jax.random.normal(own_key, dims, jnp.float32)
    if cuts:
        result = result * level_of(own_key, dims, cuts, -0.22, 0.18)
    return jnp.clip(result, -limit, limit).astype(kind)


def setup_inputs(seed: int = 0, part: int = 0) -> dict:
    arg_keys = jax.random.split(jax.random.key(seed), 8)
    part_keys = jax.random.split(jax.random.fold_in(arg_keys[7], part), 8)
    patterns = noise(part_keys[0], (SY, KD, SX), 1.0, 6.0, ((0, 4), (1, 4)), jnp.float32)
    jitter = with_ends(jax.random.randint(part_keys[1], (SY,), -8, 9), jax.random.fold_in(part_keys[1], 1), -8, 8).astype(jnp.int32)
    subpixel = with_ends(jax.random.randint(part_keys[2], (SY,), 0, NPHASE), jax.random.fold_in(part_keys[2], 1), 0, NPHASE - 1).astype(jnp.int32)
    kernels = noise(arg_keys[3], (NPHASE, TAPS), 0.6, 3.0, (), jnp.float32)
    intersection = with_ends((jax.random.randint(arg_keys[4], (DS, SY, N_ROW), 0, 4) < 3).astype(jnp.int32), jax.random.fold_in(arg_keys[4], 1), 0, 1)
    owners_keys = jax.random.split(jax.random.fold_in(arg_keys[5], 1), DS * SY // SY)
    owners_turns = jax.random.permutation(jax.random.fold_in(arg_keys[5], 3), DS * SY // SY)
    owners = jax.vmap(lambda own, number: routed_block(jax.random.fold_in(arg_keys[5], 2), own, number, SY, N_ROW, 1, CAP, 2))(owners_keys, owners_turns).reshape((DS, SY, 1))
    wigner = noise(arg_keys[6], (2, KY, KX), 1.0, 6.0, (), jnp.float32)
    return dict(patterns=patterns, jitter=jitter, subpixel=subpixel, kernels=kernels, intersection=intersection, owners=owners, wigner=wigner)


def slot_table(column, owners_count, capacity):
    positions = jnp.arange(column.shape[0], dtype=jnp.int32)
    earlier = (column[:, None] == column[None, :]) & (positions[:, None] < positions[None, :])
    ranking = lax.optimization_barrier(jnp.sum(earlier.astype(jnp.int32), axis=0))
    matches = (column[None, None, :] == jnp.arange(owners_count, dtype=jnp.int32)[:, None, None]) & (ranking[None, None, :] == jnp.arange(capacity, dtype=jnp.int32)[None, :, None])
    chosen = lax.optimization_barrier(jnp.sum(jnp.where(matches, positions[None, None, :], 0), axis=-1)).astype(jnp.int32)
    filled = jnp.any(matches, axis=-1)
    return (chosen, filled)

def reference(patterns, jitter, subpixel, kernels, intersection, owners, wigner):
    centre = TAPS // 2
    samples = jnp.arange(SX, dtype=jnp.int32)
    weights = kernels[subpixel]
    dejittered = jnp.zeros(patterns.shape, jnp.float32)
    for offset in range(TAPS):
        indices = jnp.mod(samples[None, :] + jitter[:, None] + (offset - centre), SX).astype(jnp.int32)
        shifted = jnp.take_along_axis(patterns, jnp.broadcast_to(indices[:, None, :], patterns.shape), axis=2)
        dejittered = dejittered + weights[:, offset][:, None, None] * shifted
    spectrum = jnp.fft.fft(jnp.fft.fft(dejittered, axis=2), axis=0) / math.sqrt(SY * SX)
    columnwise = jnp.transpose(spectrum.reshape(SY, KD, DS, SXS), (2, 0, 1, 3))
    visible = jnp.repeat(intersection, PB, axis=2).astype(jnp.float32)
    masked = columnwise * visible[..., None]
    transformed = jnp.fft.fft2(masked.reshape(DS, SY, KY, KX, SXS), axes=(2, 3)) / math.sqrt(KD)
    denominator = wigner[0] * wigner[0] + wigner[1] * wigner[1] + 0.1
    wiener = (wigner[0] - 1j * wigner[1]) / denominator
    folded = lax.optimization_barrier(jnp.sum(wiener[None, None, :, :, None] * transformed, axis=3)) / math.sqrt(KX)
    layout = jnp.concatenate([jnp.real(folded), jnp.imag(folded)], axis=3).astype(jnp.float32)
    chosen, filled = jax.vmap(slot_table, in_axes=(0, None, None))(owners[:, :, 0], N_ROW, CAP)
    flattened = layout.reshape(DS * SY, KY, 2 * SXS)
    offsets = (jnp.arange(DS, dtype=jnp.int32) * SY)[:, None, None]
    picked = jnp.take(flattened, (chosen + offsets).reshape(-1), axis=0)
    picked = picked.reshape(DS, N_ROW, CAP, KY, 2 * SXS)
    return jnp.where(filled[..., None, None], picked, 0.0).astype(jnp.float32)
```

```python
import functools
import math

import jax
import jax.numpy as jnp
import numpy as np
from jax import lax
from jax.experimental import pallas as pl
from jax.experimental.pallas import tpu as pltpu
from jax.sharding import PartitionSpec as P

CAP = 2
SHIFTS = 32

highest = lax.Precision.HIGHEST
f32 = jnp.float32
bf16 = jnp.bfloat16


def slot_table(column, owners_count, capacity):
    positions = jnp.arange(column.shape[0], dtype=jnp.int32)
    earlier = (column[:, None] == column[None, :]) & (positions[:, None] < positions[None, :])
    ranking = jnp.sum(earlier.astype(jnp.int32), axis=0)
    matches = (
        column[None, None, :] == jnp.arange(owners_count, dtype=jnp.int32)[:, None, None]
    ) & (ranking[None, None, :] == jnp.arange(capacity, dtype=jnp.int32)[None, :, None])
    return matches.astype(f32)


def unit_circle(products, length):
    angles = 2.0 * np.pi / length * np.mod(products, length)
    return np.cos(angles), np.sin(angles)


def fast_tables(length, groups, scan_rows):
    samples = np.arange(length)
    cosine, sine = unit_circle(samples[:, None] * samples[None, :], length)
    scale = 1.0 / math.sqrt(length * scan_rows)
    both = np.stack([cosine, sine]).reshape(2, length, groups, length // groups)
    return (both.transpose(2, 1, 0, 3) * scale).reshape(groups, length, -1).astype(np.float32)


def inner_table(width, repeats):
    index = np.arange(width)
    cosine, sine = unit_circle(index[:, None] * index[None, :], width)
    return np.concatenate([np.tile(cosine, repeats), np.tile(sine, repeats)], 1).astype(np.float32)


def row_tables(height, width, groups):
    pixels = np.arange(height * width)
    cosine, sine = unit_circle(np.arange(height)[:, None] * (pixels // width)[None, :], height)
    both = np.stack([cosine, sine]) / math.sqrt(height * width * width)
    return both.reshape(2, height, groups, -1).transpose(2, 0, 1, 3).astype(np.float32)


def shift_tables(length, groups):
    shifts = np.arange(SHIFTS) - SHIFTS // 2
    cosine, sine = unit_circle(shifts[:, None] * np.arange(length)[None, :], length)
    both = np.stack([cosine, sine]).reshape(2, SHIFTS, groups, length // groups)
    return both.transpose(2, 0, 1, 3).astype(np.float32)


def wiener_parts(real, imaginary):
    denominator = real * real + imaginary * imaginary + 0.1
    return real / denominator, -imaginary / denominator


def general(patterns, jitter, subpixel, kernels, intersection, owners, wigner):
    _, pixel_share, length = patterns.shape
    height, width = wigner.shape[1:]
    groups = lax.axis_size(("det", "sub"))
    rows = lax.axis_size("row")
    columns = length // groups
    block_pixels = pixel_share * groups // rows
    local_blocks = pixel_share // block_pixels
    scan_rows = owners.shape[1]
    group = lax.axis_index(("det", "sub"))
    dot = functools.partial(jnp.einsum, precision=highest)

    filter_real, filter_imaginary = wiener_parts(wigner[0], wigner[1])
    repeats = pixel_share // width
    table = jnp.asarray(inner_table(width, 1))
    cosine, sine = table[:, :width], table[:, width:]
    inner_real = dot("rx,xk->rk", filter_real, cosine) + dot("rx,xk->rk", filter_imaginary, sine)
    inner_imaginary = dot("rx,xk->rk", filter_imaginary, cosine) - dot("rx,xk->rk", filter_real, sine)
    inner_real, inner_imaginary = (jnp.tile(v, (1, repeats)) for v in (inner_real, inner_imaginary))
    turn = lax.dynamic_index_in_dim(jnp.asarray(row_tables(height, width, groups)), group, 0, False)
    matrix = jnp.concatenate(
        [inner_real * turn[0] + inner_imaginary * turn[1], inner_imaginary * turn[0] - inner_real * turn[1]]
    )
    folded = dot(
        "rnp,npx->nrx",
        matrix.reshape(2 * height, local_blocks, block_pixels),
        patterns[0].reshape(local_blocks, block_pixels, length),
    )
    selector = (jnp.arange(kernels.shape[0], dtype=jnp.int32) == subpixel[0]).astype(f32)
    weights = dot("k,kt->t", selector, kernels)
    taps = kernels.shape[1]
    moved = sum(
        weights[t] * jnp.roll(folded, -(jitter[0] + t - taps // 2), axis=2) for t in range(taps)
    )
    spectrum = dot("nrx,gxf->gnrf", moved, jnp.asarray(fast_tables(length, groups, scan_rows)))
    upper, lower = spectrum[:, :, :height], spectrum[:, :, height:]
    spectrum = jnp.concatenate(
        [upper[..., :columns] + lower[..., columns:], lower[..., :columns] - upper[..., columns:]], 3
    )
    gathered = lax.all_to_all(spectrum, ("det", "sub"), split_axis=0, concat_axis=1, tiled=True)[0]
    visible = lax.all_gather(intersection[0], "row", axis=1, tiled=True).astype(f32)
    masked = dot("qb,brf->qrf", visible, gathered)
    cosine, sine = unit_circle(np.arange(scan_rows)[:, None] * np.arange(rows)[None, :], rows)
    me = lax.axis_index("row")
    cosine = jnp.asarray(cosine, f32)[:, me][:, None, None]
    sine = jnp.asarray(sine, f32)[:, me][:, None, None]
    real, imaginary = masked[..., :columns], masked[..., columns:]
    turned = jnp.concatenate([cosine * real + sine * imaginary, cosine * imaginary - sine * real], 2)
    slots = dot("ocq,qrf->ocrf", slot_table(owners[0, :, 0], rows, CAP), turned)
    return lax.psum_scatter(slots, "row", scatter_dimension=0, tiled=True)[None]


def split(value):
    high = value.astype(bf16)
    return high, (value - high.astype(f32)).astype(bf16)


def times(a, b):
    return jnp.dot(a, b, preferred_element_type=f32)


def scaled(factor, value):
    if abs(factor) < 1e-9:
        return None
    if abs(factor - 1.0) < 1e-9:
        return value
    return value * np.float32(factor)


def added(terms):
    terms = [term for term in terms if term is not None]
    return functools.reduce(lambda a, b: a + b, terms)


def fused_kernel(
    sizes, patterns, jitter, subpixel, kernels, intersection, owners, wigner, inner, turns,
    fast_high, fast_low, phases, out, pixels, turn, table_high, table_low, outgoing, incoming,
    visible, slots, load_sem, send_sem, recv_sem, mask_send, mask_recv, slot_send, slot_recv,
):
    rows, groups, subs, scan_rows, height, columns, chunks = sizes
    row = lax.axis_index("row")
    group = lax.axis_index("det") * subs + lax.axis_index("sub")
    part = height // rows
    peers = [(dr, dg) for dg in range(groups) for dr in range(rows) if (dr, dg) != (0, 0)]

    def row_at(offset):
        return lax.rem(row + offset, rows)

    def group_at(offset):
        return lax.rem(group + offset, groups)

    def device(dr, dg):
        other = group_at(dg)
        return {"row": row_at(dr), "det": other // subs, "sub": lax.rem(other, subs)}

    def rows_of(index):
        return pl.ds(pl.multiple_of(index * part, part), part)

    chunk = pixels.shape[0] // chunks
    loads = [
        pltpu.make_async_copy(turns.at[group], turn, load_sem.at[0]),
        pltpu.make_async_copy(fast_high, table_high, load_sem.at[1]),
        pltpu.make_async_copy(fast_low, table_low, load_sem.at[2]),
    ]
    pieces = [
        pltpu.make_async_copy(
            patterns.at[0, pl.ds(k * chunk, chunk)], pixels.at[pl.ds(k * chunk, chunk)], load_sem.at[3 + k]
        )
        for k in range(chunks)
    ]
    loads[0].start()
    for piece in pieces:
        piece.start()
    loads[1].start()
    loads[2].start()

    barrier = pltpu.get_barrier_semaphore()
    for dr, dg in peers:
        pl.semaphore_signal(
            barrier, inc=1, device_id=device(dr, dg), device_id_type=pl.DeviceIdType.MESH
        )

    filter_real, filter_imaginary = wiener_parts(wigner[0], wigner[1])
    both = jnp.dot(
        jnp.concatenate([filter_real, filter_imaginary]), inner[...],
        precision=highest, preferred_element_type=f32,
    )
    lanes = inner.shape[1] // 2
    inner_real = both[:height, :lanes] + both[height:, lanes:]
    inner_imaginary = both[height:, :lanes] - both[:height, lanes:]
    loads[0].wait()
    matrix = []
    for k in range(pixels.shape[0] // lanes):
        cosine = turn[0, :, k * lanes : (k + 1) * lanes]
        sine = turn[1, :, k * lanes : (k + 1) * lanes]
        matrix.append(
            split(
                jnp.concatenate(
                    [inner_real * cosine + inner_imaginary * sine, inner_imaginary * cosine - inner_real * sine]
                )
            )
        )
    per_chunk = chunk // lanes
    folded = jnp.zeros((2 * height, pixels.shape[1]), f32)
    for k in range(chunks):
        mine = matrix[k * per_chunk : (k + 1) * per_chunk]
        high = jnp.concatenate([m[0] for m in mine], 1)
        low = jnp.concatenate([m[1] for m in mine], 1)
        pieces[k].wait()
        piece_high, piece_low = split(pixels[k * chunk : (k + 1) * chunk, :])
        folded = folded + (times(high, piece_high) + times(high, piece_low) + times(low, piece_high))
    folded_high, folded_low = split(folded)

    shifts = lax.broadcasted_iota(jnp.int32, (SHIFTS, columns), 0) - SHIFTS // 2
    taps = kernels.shape[1]
    weight = jnp.zeros((SHIFTS, columns), f32)
    for t in range(taps):
        weight = weight + jnp.where(
            shifts == jitter[0] + (t - taps // 2), kernels[subpixel[0], t], 0.0
        )

    frequency = lax.broadcasted_iota(jnp.int32, visible.shape[1:], 0)
    tile = jnp.zeros(visible.shape[1:], f32)
    for q in range(scan_rows):
        tile = jnp.where(frequency == q, intersection[0, q, 0].astype(f32), tile)
    visible[row] = tile

    pl.semaphore_wait(barrier, len(peers))
    masks = []
    for dr in range(1, rows):
        copy = pltpu.make_async_remote_copy(
            src_ref=visible.at[row], dst_ref=visible.at[row], send_sem=mask_send.at[dr],
            recv_sem=mask_recv.at[row], device_id=device(dr, 0), device_id_type=pl.DeviceIdType.MESH,
        )
        copy.start()
        masks.append(copy)

    loads[1].wait()
    loads[2].wait()
    sends = []
    for dg in list(range(1, groups)) + [0]:
        other = group_at(dg)
        high = table_high[other]
        product = times(folded_high, high) + times(folded_high, table_low[other]) + times(folded_low, high)
        real = product[:height, :columns] + product[height:, columns:]
        imaginary = product[height:, :columns] - product[:height, columns:]
        phase_real = jnp.sum(weight * phases[other, 0], axis=0, keepdims=True)
        phase_imaginary = jnp.sum(weight * phases[other, 1], axis=0, keepdims=True)
        outgoing[dg, :, :columns] = real * phase_real - imaginary * phase_imaginary
        outgoing[dg, :, columns:] = real * phase_imaginary + imaginary * phase_real
        for dr in range(rows):
            if (dr, dg) == (0, 0):
                incoming[row, group] = outgoing[0, rows_of(row), :]
                continue
            copy = pltpu.make_async_remote_copy(
                src_ref=outgoing.at[dg, rows_of(row_at(dr)), :], dst_ref=incoming.at[row, group],
                send_sem=send_sem.at[dr, dg], recv_sem=recv_sem.at[row, group],
                device_id=device(dr, dg), device_id_type=pl.DeviceIdType.MESH,
            )
            copy.start()
            sends.append(copy)

    for dr in range(1, rows):
        pltpu.make_async_remote_copy(
            src_ref=visible.at[row_at(dr)], dst_ref=visible.at[row_at(dr)], send_sem=mask_send.at[dr],
            recv_sem=mask_recv.at[row_at(dr)], device_id=device(dr, 0), device_id_type=pl.DeviceIdType.MESH,
        ).wait_recv()
    for dr, dg in peers:
        pltpu.make_async_remote_copy(
            src_ref=outgoing.at[dg, rows_of(row), :], dst_ref=incoming.at[row_at(dr), group_at(dg)],
            send_sem=send_sem.at[dr, dg], recv_sem=recv_sem.at[row_at(dr), group_at(dg)],
            device_id=device(dr, dg), device_id_type=pl.DeviceIdType.MESH,
        ).wait_recv()

    real = [None] * scan_rows
    imaginary = [None] * scan_rows
    for b in range(groups):
        values = [incoming[y, b] for y in range(rows)]
        reals = [v[:, :columns] for v in values]
        imaginaries = [v[:, columns:] for v in values]
        for q in range(scan_rows):
            circle = [unit_circle(np.array(q * y), rows) for y in range(rows)]
            keep = visible[b, q : q + 1, :]
            sum_real = added(
                [scaled(c, v) for (c, _), v in zip(circle, reals)]
                + [scaled(s, v) for (_, s), v in zip(circle, imaginaries)]
            )
            sum_imaginary = added(
                [scaled(c, v) for (c, _), v in zip(circle, imaginaries)]
                + [scaled(-s, v) for (_, s), v in zip(circle, reals)]
            )
            real[q] = added([real[q], keep * sum_real])
            imaginary[q] = added([imaginary[q], keep * sum_imaginary])

    owner = [owners[0, q, 0] for q in range(scan_rows)]
    ranking = [
        sum([(owner[p] == owner[q]).astype(jnp.int32) for p in range(q)], jnp.int32(0))
        for q in range(scan_rows)
    ]
    slot_copies = []
    for dr in list(range(1, rows)) + [0]:
        target = row_at(dr)
        for c in range(CAP):
            chosen = [
                jnp.where((owner[q] == target) & (ranking[q] == c), 1.0, 0.0).astype(f32)
                for q in range(scan_rows)
            ]
            slot_real = added([chosen[q] * real[q] for q in range(scan_rows)])
            slot_imaginary = added([chosen[q] * imaginary[q] for q in range(scan_rows)])
            if dr == 0:
                out[0, 0, c, rows_of(row), :columns] = slot_real
                out[0, 0, c, rows_of(row), columns:] = slot_imaginary
            else:
                slots[dr, c, :, :columns] = slot_real
                slots[dr, c, :, columns:] = slot_imaginary
        if dr:
            copy = pltpu.make_async_remote_copy(
                src_ref=slots.at[dr], dst_ref=out.at[0, 0, :, rows_of(row), :],
                send_sem=slot_send.at[dr], recv_sem=slot_recv.at[row],
                device_id=device(dr, 0), device_id_type=pl.DeviceIdType.MESH,
            )
            copy.start()
            slot_copies.append(copy)

    for dr in range(1, rows):
        pltpu.make_async_remote_copy(
            src_ref=slots.at[dr], dst_ref=out.at[0, 0, :, rows_of(row_at(dr)), :],
            send_sem=slot_send.at[dr], recv_sem=slot_recv.at[row_at(dr)],
            device_id=device(dr, 0), device_id_type=pl.DeviceIdType.MESH,
        ).wait_recv()
    for copy in masks + sends + slot_copies:
        copy.wait_send()


def fused(patterns, jitter, subpixel, kernels, intersection, owners, wigner):
    _, pixel_share, length = patterns.shape
    height, width = wigner.shape[1:]
    subs = lax.axis_size("sub")
    groups = lax.axis_size("det") * subs
    rows = lax.axis_size("row")
    columns = length // groups
    scan_rows = owners.shape[1]
    part = height // rows
    chunks = 4
    fast = fast_tables(length, groups, scan_rows)
    fast_high = fast.astype(bf16)
    fast_low = (fast - fast_high.astype(np.float32)).astype(bf16)
    vmem = pl.BlockSpec(memory_space=pltpu.VMEM)
    smem = pl.BlockSpec(memory_space=pltpu.SMEM)
    hbm = pl.BlockSpec(memory_space=pl.ANY)
    sizes = (rows, groups, subs, scan_rows, height, columns, chunks)
    mask_rows = -(-scan_rows // 8) * 8
    dma = pltpu.SemaphoreType.DMA
    return pl.pallas_call(
        functools.partial(fused_kernel, sizes),
        out_shape=jax.ShapeDtypeStruct((1, 1, CAP, height, 2 * columns), f32),
        in_specs=[hbm, smem, smem, smem, smem, smem, vmem, vmem, hbm, hbm, hbm, vmem],
        out_specs=vmem,
        scratch_shapes=[
            pltpu.VMEM((pixel_share, length), f32),
            pltpu.VMEM((2, height, pixel_share), f32),
            pltpu.VMEM((groups, length, 2 * columns), bf16),
            pltpu.VMEM((groups, length, 2 * columns), bf16),
            pltpu.VMEM((groups, height, 2 * columns), f32),
            pltpu.VMEM((rows, groups, part, 2 * columns), f32),
            pltpu.VMEM((rows, mask_rows, columns), f32),
            pltpu.VMEM((rows, CAP, part, 2 * columns), f32),
            dma((3 + chunks,)),
            dma((rows, groups)),
            dma((rows, groups)),
            dma((rows,)),
            dma((rows,)),
            dma((rows,)),
            dma((rows,)),
        ],
        compiler_params=pltpu.CompilerParams(
            collective_id=0, has_side_effects=True, vmem_limit_bytes=32 * 1024 * 1024
        ),
    )(
        patterns, jitter, subpixel, kernels, intersection, owners, wigner,
        jnp.asarray(inner_table(width, 128 // width)),
        jnp.asarray(row_tables(height, width, groups)),
        jnp.asarray(fast_high), jnp.asarray(fast_low),
        jnp.asarray(shift_tables(length, groups)),
    )


def per_device(patterns, jitter, subpixel, kernels, intersection, owners, wigner):
    _, pixel_share, length = patterns.shape
    height, width = wigner.shape[1:]
    groups = lax.axis_size(("det", "sub"))
    rows = lax.axis_size("row")
    one_block = groups == rows and pixel_share % 1024 == 0
    tiles = height % (8 * rows) == 0 and (length // groups) % 128 == 0 and 128 % width == 0
    form = fused if one_block and tiles else general
    return form(patterns, jitter, subpixel, kernels, intersection, owners, wigner)


def solution(mesh):
    return jax.shard_map(
        per_device,
        mesh=mesh,
        in_specs=(
            P(("grp", "row"), ("det", "sub"), None),
            P(("grp", "row")),
            P(("grp", "row")),
            P(),
            P(("det", "sub"), None, "row"),
            P(("det", "sub"), None, None),
            P(),
        ),
        out_specs=P(("grp", "det", "sub"), "row", None, None, None),
        check_vma=False,
    )
```

```python
import functools
import math

import jax
import jax.numpy as jnp
import numpy as np
from jax import lax
from jax.experimental import pallas as pl
from jax.experimental.pallas import tpu as pltpu
from jax.sharding import PartitionSpec as P

CAP = 2
SHIFTS = 32

highest = lax.Precision.HIGHEST
f32 = jnp.float32
bf16 = jnp.bfloat16


def slot_table(column, owners_count, capacity):
    positions = jnp.arange(column.shape[0], dtype=jnp.int32)
    earlier = (column[:, None] == column[None, :]) & (positions[:, None] < positions[None, :])
    ranking = jnp.sum(earlier.astype(jnp.int32), axis=0)
    matches = (
        column[None, None, :] == jnp.arange(owners_count, dtype=jnp.int32)[:, None, None]
    ) & (ranking[None, None, :] == jnp.arange(capacity, dtype=jnp.int32)[None, :, None])
    return matches.astype(f32)


def unit_circle(products, length):
    angles = 2.0 * np.pi / length * np.mod(products, length)
    return np.cos(angles), np.sin(angles)


def fast_tables(length, groups, scan_rows):
    samples = np.arange(length)
    cosine, sine = unit_circle(samples[:, None] * samples[None, :], length)
    scale = 1.0 / math.sqrt(length * scan_rows)
    both = np.stack([cosine, sine]).reshape(2, length, groups, length // groups)
    return (both.transpose(2, 1, 0, 3) * scale).reshape(groups, length, -1).astype(np.float32)


def inner_table(width, repeats):
    index = np.arange(width)
    cosine, sine = unit_circle(index[:, None] * index[None, :], width)
    return np.concatenate([np.tile(cosine, repeats), np.tile(sine, repeats)], 1).astype(np.float32)


def row_tables(height, width, groups):
    pixels = np.arange(height * width)
    cosine, sine = unit_circle(np.arange(height)[:, None] * (pixels // width)[None, :], height)
    both = np.stack([cosine, sine]) / math.sqrt(height * width * width)
    return both.reshape(2, height, groups, -1).transpose(2, 0, 1, 3).astype(np.float32)


def shift_tables(length, groups):
    shifts = np.arange(SHIFTS) - SHIFTS // 2
    cosine, sine = unit_circle(shifts[:, None] * np.arange(length)[None, :], length)
    both = np.stack([cosine, sine]).reshape(2, SHIFTS, groups, length // groups)
    return both.transpose(2, 0, 1, 3).astype(np.float32)


def wiener_parts(real, imaginary):
    denominator = real * real + imaginary * imaginary + 0.1
    return real / denominator, -imaginary / denominator


def general(patterns, jitter, subpixel, kernels, intersection, owners, wigner):
    _, pixel_share, length = patterns.shape
    height, width = wigner.shape[1:]
    groups = lax.axis_size(("det", "sub"))
    rows = lax.axis_size("row")
    columns = length // groups
    block_pixels = pixel_share * groups // rows
    local_blocks = pixel_share // block_pixels
    scan_rows = owners.shape[1]
    group = lax.axis_index(("det", "sub"))
    dot = functools.partial(jnp.einsum, precision=highest)

    filter_real, filter_imaginary = wiener_parts(wigner[0], wigner[1])
    repeats = pixel_share // width
    table = jnp.asarray(inner_table(width, 1))
    cosine, sine = table[:, :width], table[:, width:]
    inner_real = dot("rx,xk->rk", filter_real, cosine) + dot("rx,xk->rk", filter_imaginary, sine)
    inner_imaginary = dot("rx,xk->rk", filter_imaginary, cosine) - dot("rx,xk->rk", filter_real, sine)
    inner_real, inner_imaginary = (jnp.tile(v, (1, repeats)) for v in (inner_real, inner_imaginary))
    turn = lax.dynamic_index_in_dim(jnp.asarray(row_tables(height, width, groups)), group, 0, False)
    matrix = jnp.concatenate(
        [inner_real * turn[0] + inner_imaginary * turn[1], inner_imaginary * turn[0] - inner_real * turn[1]]
    )
    folded = dot(
        "rnp,npx->nrx",
        matrix.reshape(2 * height, local_blocks, block_pixels),
        patterns[0].reshape(local_blocks, block_pixels, length),
    )
    selector = (jnp.arange(kernels.shape[0], dtype=jnp.int32) == subpixel[0]).astype(f32)
    weights = dot("k,kt->t", selector, kernels)
    taps = kernels.shape[1]
    moved = sum(
        weights[t] * jnp.roll(folded, -(jitter[0] + t - taps // 2), axis=2) for t in range(taps)
    )
    spectrum = dot("nrx,gxf->gnrf", moved, jnp.asarray(fast_tables(length, groups, scan_rows)))
    upper, lower = spectrum[:, :, :height], spectrum[:, :, height:]
    spectrum = jnp.concatenate(
        [upper[..., :columns] + lower[..., columns:], lower[..., :columns] - upper[..., columns:]], 3
    )
    gathered = lax.all_to_all(spectrum, ("det", "sub"), split_axis=0, concat_axis=1, tiled=True)[0]
    visible = lax.all_gather(intersection[0], "row", axis=1, tiled=True).astype(f32)
    masked = dot("qb,brf->qrf", visible, gathered)
    cosine, sine = unit_circle(np.arange(scan_rows)[:, None] * np.arange(rows)[None, :], rows)
    me = lax.axis_index("row")
    cosine = jnp.asarray(cosine, f32)[:, me][:, None, None]
    sine = jnp.asarray(sine, f32)[:, me][:, None, None]
    real, imaginary = masked[..., :columns], masked[..., columns:]
    turned = jnp.concatenate([cosine * real + sine * imaginary, cosine * imaginary - sine * real], 2)
    slots = dot("ocq,qrf->ocrf", slot_table(owners[0, :, 0], rows, CAP), turned)
    return lax.psum_scatter(slots, "row", scatter_dimension=0, tiled=True)[None]


def split(value):
    high = value.astype(bf16)
    return high, (value - high.astype(f32)).astype(bf16)


def times(a, b):
    return jnp.dot(a, b, preferred_element_type=f32)


def scaled(factor, value):
    if abs(factor) < 1e-9:
        return None
    if abs(factor - 1.0) < 1e-9:
        return value
    return value * np.float32(factor)


def added(terms):
    terms = [term for term in terms if term is not None]
    return functools.reduce(lambda a, b: a + b, terms)


def fused_kernel(
    sizes, patterns, jitter, subpixel, kernels, intersection, owners, wigner, inner, turns,
    fast_high, fast_low, phases, out, kernels_here, intersection_here,
    owners_here, wigner_here, inner_here, phases_here, pixels, turn, table_high, table_low, outgoing,
    incoming, visible, slots, small_sem, load_sem, send_sem, recv_sem, mask_send, mask_recv,
    slot_send, slot_recv,
):
    rows, groups, subs, scan_rows, height, columns, chunks = sizes
    row = lax.axis_index("row")
    group = lax.axis_index("det") * subs + lax.axis_index("sub")
    part = height // rows
    peers = [(dr, dg) for dg in range(groups) for dr in range(rows) if (dr, dg) != (0, 0)]

    def row_at(offset):
        return lax.rem(row + offset, rows)

    def group_at(offset):
        return lax.rem(group + offset, groups)

    def device(dr, dg):
        other = group_at(dg)
        return {"row": row_at(dr), "det": other // subs, "sub": lax.rem(other, subs)}

    def rows_of(index):
        return pl.ds(pl.multiple_of(index * part, part), part)

    chunk = pixels.shape[0] // chunks
    loads = [
        pltpu.make_async_copy(turns.at[group], turn, load_sem.at[0]),
        pltpu.make_async_copy(fast_high, table_high, load_sem.at[1]),
        pltpu.make_async_copy(fast_low, table_low, load_sem.at[2]),
    ]
    pieces = [
        pltpu.make_async_copy(
            patterns.at[0, pl.ds(k * chunk, chunk)], pixels.at[pl.ds(k * chunk, chunk)], load_sem.at[3 + k]
        )
        for k in range(chunks)
    ]
    small = [
        pltpu.make_async_copy(source, target, small_sem.at[k])
        for k, (source, target) in enumerate(
            [
                (wigner, wigner_here), (inner, inner_here), (kernels, kernels_here),
                (intersection, intersection_here), (owners, owners_here), (phases, phases_here),
            ]
        )
    ]
    for copy in small:
        copy.start()
    loads[0].start()
    for piece in pieces:
        piece.start()
    loads[1].start()
    loads[2].start()

    barrier = pltpu.get_barrier_semaphore()
    for dr, dg in peers:
        pl.semaphore_signal(
            barrier, inc=1, device_id=device(dr, dg), device_id_type=pl.DeviceIdType.MESH
        )

    small[0].wait()
    small[1].wait()
    filter_real, filter_imaginary = wiener_parts(wigner_here[0], wigner_here[1])
    both = jnp.dot(
        jnp.concatenate([filter_real, filter_imaginary]), inner_here[...],
        precision=highest, preferred_element_type=f32,
    )
    lanes = inner_here.shape[1] // 2
    inner_real = both[:height, :lanes] + both[height:, lanes:]
    inner_imaginary = both[height:, :lanes] - both[:height, lanes:]
    loads[0].wait()
    matrix = []
    for k in range(pixels.shape[0] // lanes):
        cosine = turn[0, :, k * lanes : (k + 1) * lanes]
        sine = turn[1, :, k * lanes : (k + 1) * lanes]
        matrix.append(
            split(
                jnp.concatenate(
                    [inner_real * cosine + inner_imaginary * sine, inner_imaginary * cosine - inner_real * sine]
                )
            )
        )
    per_chunk = chunk // lanes
    folded = jnp.zeros((2 * height, pixels.shape[1]), f32)
    for k in range(chunks):
        mine = matrix[k * per_chunk : (k + 1) * per_chunk]
        high = jnp.concatenate([m[0] for m in mine], 1)
        low = jnp.concatenate([m[1] for m in mine], 1)
        pieces[k].wait()
        piece_high, piece_low = split(pixels[k * chunk : (k + 1) * chunk, :])
        folded = folded + (times(high, piece_high) + times(high, piece_low) + times(low, piece_high))
    folded_high, folded_low = split(folded)

    for copy in small[2:]:
        copy.wait()
    shifts = lax.broadcasted_iota(jnp.int32, (SHIFTS, columns), 0) - SHIFTS // 2
    taps = kernels.shape[0]
    weight = jnp.zeros((SHIFTS, columns), f32)
    for t in range(taps):
        weight = weight + jnp.where(
            shifts == jitter[0] + (t - taps // 2), kernels_here[t, subpixel[0]], 0.0
        )

    frequency = lax.broadcasted_iota(jnp.int32, visible.shape[1:], 0)
    tile = jnp.zeros(visible.shape[1:], f32)
    for q in range(scan_rows):
        tile = jnp.where(frequency == q, intersection_here[0, q].astype(f32), tile)
    visible[row] = tile

    pl.semaphore_wait(barrier, len(peers))
    masks = []
    for dr in range(1, rows):
        copy = pltpu.make_async_remote_copy(
            src_ref=visible.at[row], dst_ref=visible.at[row], send_sem=mask_send.at[dr],
            recv_sem=mask_recv.at[row], device_id=device(dr, 0), device_id_type=pl.DeviceIdType.MESH,
        )
        copy.start()
        masks.append(copy)

    loads[1].wait()
    loads[2].wait()
    sends = []
    for dg in list(range(1, groups)) + [0]:
        other = group_at(dg)
        high = table_high[other]
        product = times(folded_high, high) + times(folded_high, table_low[other]) + times(folded_low, high)
        real = product[:height, :columns] + product[height:, columns:]
        imaginary = product[height:, :columns] - product[:height, columns:]
        phase_real = jnp.sum(weight * phases_here[other, 0], axis=0, keepdims=True)
        phase_imaginary = jnp.sum(weight * phases_here[other, 1], axis=0, keepdims=True)
        outgoing[dg, :, :columns] = real * phase_real - imaginary * phase_imaginary
        outgoing[dg, :, columns:] = real * phase_imaginary + imaginary * phase_real
        for dr in range(rows):
            if (dr, dg) == (0, 0):
                incoming[row, group] = outgoing[0, rows_of(row), :]
                continue
            copy = pltpu.make_async_remote_copy(
                src_ref=outgoing.at[dg, rows_of(row_at(dr)), :], dst_ref=incoming.at[row, group],
                send_sem=send_sem.at[dr, dg], recv_sem=recv_sem.at[row, group],
                device_id=device(dr, dg), device_id_type=pl.DeviceIdType.MESH,
            )
            copy.start()
            sends.append(copy)

    for dr in range(1, rows):
        pltpu.make_async_remote_copy(
            src_ref=visible.at[row_at(dr)], dst_ref=visible.at[row_at(dr)], send_sem=mask_send.at[dr],
            recv_sem=mask_recv.at[row_at(dr)], device_id=device(dr, 0), device_id_type=pl.DeviceIdType.MESH,
        ).wait_recv()
    for dr, dg in peers:
        pltpu.make_async_remote_copy(
            src_ref=outgoing.at[dg, rows_of(row), :], dst_ref=incoming.at[row_at(dr), group_at(dg)],
            send_sem=send_sem.at[dr, dg], recv_sem=recv_sem.at[row_at(dr), group_at(dg)],
            device_id=device(dr, dg), device_id_type=pl.DeviceIdType.MESH,
        ).wait_recv()

    real = [None] * scan_rows
    imaginary = [None] * scan_rows
    for b in range(groups):
        values = [incoming[y, b] for y in range(rows)]
        reals = [v[:, :columns] for v in values]
        imaginaries = [v[:, columns:] for v in values]
        for q in range(scan_rows):
            circle = [unit_circle(np.array(q * y), rows) for y in range(rows)]
            keep = visible[b, q : q + 1, :]
            sum_real = added(
                [scaled(c, v) for (c, _), v in zip(circle, reals)]
                + [scaled(s, v) for (_, s), v in zip(circle, imaginaries)]
            )
            sum_imaginary = added(
                [scaled(c, v) for (c, _), v in zip(circle, imaginaries)]
                + [scaled(-s, v) for (_, s), v in zip(circle, reals)]
            )
            real[q] = added([real[q], keep * sum_real])
            imaginary[q] = added([imaginary[q], keep * sum_imaginary])

    owner = [owners_here[0, q] for q in range(scan_rows)]
    ranking = [
        sum([(owner[p] == owner[q]).astype(jnp.int32) for p in range(q)], jnp.int32(0))
        for q in range(scan_rows)
    ]
    slot_copies = []
    for dr in list(range(1, rows)) + [0]:
        target = row_at(dr)
        for c in range(CAP):
            chosen = [
                jnp.where((owner[q] == target) & (ranking[q] == c), 1.0, 0.0).astype(f32)
                for q in range(scan_rows)
            ]
            slot_real = added([chosen[q] * real[q] for q in range(scan_rows)])
            slot_imaginary = added([chosen[q] * imaginary[q] for q in range(scan_rows)])
            if dr == 0:
                out[0, 0, c, rows_of(row), :columns] = slot_real
                out[0, 0, c, rows_of(row), columns:] = slot_imaginary
            else:
                slots[dr, c, :, :columns] = slot_real
                slots[dr, c, :, columns:] = slot_imaginary
        if dr:
            copy = pltpu.make_async_remote_copy(
                src_ref=slots.at[dr], dst_ref=out.at[0, 0, :, rows_of(row), :],
                send_sem=slot_send.at[dr], recv_sem=slot_recv.at[row],
                device_id=device(dr, 0), device_id_type=pl.DeviceIdType.MESH,
            )
            copy.start()
            slot_copies.append(copy)

    for dr in range(1, rows):
        pltpu.make_async_remote_copy(
            src_ref=slots.at[dr], dst_ref=out.at[0, 0, :, rows_of(row_at(dr)), :],
            send_sem=slot_send.at[dr], recv_sem=slot_recv.at[row_at(dr)],
            device_id=device(dr, 0), device_id_type=pl.DeviceIdType.MESH,
        ).wait_recv()
    for copy in masks + sends + slot_copies:
        copy.wait_send()


def fused(patterns, jitter, subpixel, kernels, intersection, owners, wigner):
    _, pixel_share, length = patterns.shape
    height, width = wigner.shape[1:]
    subs = lax.axis_size("sub")
    groups = lax.axis_size("det") * subs
    rows = lax.axis_size("row")
    columns = length // groups
    scan_rows = owners.shape[1]
    part = height // rows
    chunks = 4
    fast = fast_tables(length, groups, scan_rows)
    fast_high = fast.astype(bf16)
    fast_low = (fast - fast_high.astype(np.float32)).astype(bf16)
    vmem = pl.BlockSpec(memory_space=pltpu.VMEM)
    smem = pl.BlockSpec(memory_space=pltpu.SMEM)
    hbm = pl.BlockSpec(memory_space=pl.ANY)
    sizes = (rows, groups, subs, scan_rows, height, columns, chunks)
    mask_rows = -(-scan_rows // 8) * 8
    dma = pltpu.SemaphoreType.DMA
    return pl.pallas_call(
        functools.partial(fused_kernel, sizes),
        out_shape=jax.ShapeDtypeStruct((1, 1, CAP, height, 2 * columns), f32),
        in_specs=[hbm, smem, smem] + [hbm] * 9,
        out_specs=vmem,
        scratch_shapes=[
            pltpu.SMEM(kernels.shape[::-1], f32),
            pltpu.SMEM((1, scan_rows), jnp.int32),
            pltpu.SMEM((1, scan_rows), jnp.int32),
            pltpu.VMEM(wigner.shape, f32),
            pltpu.VMEM((width, 256), f32),
            pltpu.VMEM((groups, 2, SHIFTS, columns), f32),
            pltpu.VMEM((pixel_share, length), f32),
            pltpu.VMEM((2, height, pixel_share), f32),
            pltpu.VMEM((groups, length, 2 * columns), bf16),
            pltpu.VMEM((groups, length, 2 * columns), bf16),
            pltpu.VMEM((groups, height, 2 * columns), f32),
            pltpu.VMEM((rows, groups, part, 2 * columns), f32),
            pltpu.VMEM((rows, mask_rows, columns), f32),
            pltpu.VMEM((rows, CAP, part, 2 * columns), f32),
            dma((6,)),
            dma((3 + chunks,)),
            dma((rows, groups)),
            dma((rows, groups)),
            dma((rows,)),
            dma((rows,)),
            dma((rows,)),
            dma((rows,)),
        ],
        compiler_params=pltpu.CompilerParams(
            collective_id=0, has_side_effects=True, vmem_limit_bytes=60 * 1024 * 1024
        ),
    )(
        patterns, jitter, subpixel, kernels.T, intersection.reshape(1, scan_rows),
        owners.reshape(1, scan_rows), wigner,
        jnp.asarray(inner_table(width, 128 // width)),
        jnp.asarray(row_tables(height, width, groups)),
        jnp.asarray(fast_high), jnp.asarray(fast_low),
        jnp.asarray(shift_tables(length, groups)),
    )


def per_device(patterns, jitter, subpixel, kernels, intersection, owners, wigner):
    _, pixel_share, length = patterns.shape
    height, width = wigner.shape[1:]
    groups = lax.axis_size(("det", "sub"))
    rows = lax.axis_size("row")
    one_block = groups == rows and pixel_share % 1024 == 0
    tiles = height % (8 * rows) == 0 and (length // groups) % 128 == 0 and 128 % width == 0
    form = fused if one_block and tiles else general
    return form(patterns, jitter, subpixel, kernels, intersection, owners, wigner)


def solution(mesh):
    return jax.shard_map(
        per_device,
        mesh=mesh,
        in_specs=(
            P(("grp", "row"), ("det", "sub"), None),
            P(("grp", "row")),
            P(("grp", "row")),
            P(),
            P(("det", "sub"), None, "row"),
            P(("det", "sub"), None, None),
            P(),
        ),
        out_specs=P(("grp", "det", "sub"), "row", None, None, None),
        check_vma=False,
    )
```

```python
import functools
import math

import jax
import jax.numpy as jnp
import numpy as np
from jax import lax
from jax.experimental import pallas as pl
from jax.experimental.pallas import tpu as pltpu
from jax.sharding import PartitionSpec as P

CAP = 2
SHIFTS = 32

highest = lax.Precision.HIGHEST
f32 = jnp.float32
bf16 = jnp.bfloat16


def slot_table(column, owners_count, capacity):
    positions = jnp.arange(column.shape[0], dtype=jnp.int32)
    earlier = (column[:, None] == column[None, :]) & (positions[:, None] < positions[None, :])
    ranking = jnp.sum(earlier.astype(jnp.int32), axis=0)
    matches = (
        column[None, None, :] == jnp.arange(owners_count, dtype=jnp.int32)[:, None, None]
    ) & (ranking[None, None, :] == jnp.arange(capacity, dtype=jnp.int32)[None, :, None])
    return matches.astype(f32)


def unit_circle(products, length):
    angles = 2.0 * np.pi / length * np.mod(products, length)
    return np.cos(angles), np.sin(angles)


def fast_tables(length, groups, scan_rows):
    samples = np.arange(length)
    cosine, sine = unit_circle(samples[:, None] * samples[None, :], length)
    scale = 1.0 / math.sqrt(length * scan_rows)
    both = np.stack([cosine, sine]).reshape(2, length, groups, length // groups)
    return (both.transpose(2, 1, 0, 3) * scale).reshape(groups, length, -1).astype(np.float32)


def inner_table(width, repeats):
    index = np.arange(width)
    cosine, sine = unit_circle(index[:, None] * index[None, :], width)
    return np.concatenate([np.tile(cosine, repeats), np.tile(sine, repeats)], 1).astype(np.float32)


def row_tables(height, width, groups):
    pixels = np.arange(height * width)
    cosine, sine = unit_circle(np.arange(height)[:, None] * (pixels // width)[None, :], height)
    both = np.stack([cosine, sine]) / math.sqrt(height * width * width)
    return both.reshape(2, height, groups, -1).transpose(2, 0, 1, 3).astype(np.float32)


def shift_tables(length, groups):
    shifts = np.arange(SHIFTS) - SHIFTS // 2
    cosine, sine = unit_circle(shifts[:, None] * np.arange(length)[None, :], length)
    both = np.stack([cosine, sine]).reshape(2, SHIFTS, groups, length // groups)
    return both.transpose(2, 0, 1, 3).astype(np.float32)


def wiener_parts(real, imaginary):
    denominator = real * real + imaginary * imaginary + 0.1
    return real / denominator, -imaginary / denominator


def general(patterns, jitter, subpixel, kernels, intersection, owners, wigner):
    _, pixel_share, length = patterns.shape
    height, width = wigner.shape[1:]
    groups = lax.axis_size(("det", "sub"))
    rows = lax.axis_size("row")
    columns = length // groups
    block_pixels = pixel_share * groups // rows
    local_blocks = pixel_share // block_pixels
    scan_rows = owners.shape[1]
    group = lax.axis_index(("det", "sub"))
    dot = functools.partial(jnp.einsum, precision=highest)

    filter_real, filter_imaginary = wiener_parts(wigner[0], wigner[1])
    repeats = pixel_share // width
    table = jnp.asarray(inner_table(width, 1))
    cosine, sine = table[:, :width], table[:, width:]
    inner_real = dot("rx,xk->rk", filter_real, cosine) + dot("rx,xk->rk", filter_imaginary, sine)
    inner_imaginary = dot("rx,xk->rk", filter_imaginary, cosine) - dot("rx,xk->rk", filter_real, sine)
    inner_real, inner_imaginary = (jnp.tile(v, (1, repeats)) for v in (inner_real, inner_imaginary))
    turn = lax.dynamic_index_in_dim(jnp.asarray(row_tables(height, width, groups)), group, 0, False)
    matrix = jnp.concatenate(
        [inner_real * turn[0] + inner_imaginary * turn[1], inner_imaginary * turn[0] - inner_real * turn[1]]
    )
    folded = dot(
        "rnp,npx->nrx",
        matrix.reshape(2 * height, local_blocks, block_pixels),
        patterns[0].reshape(local_blocks, block_pixels, length),
    )
    selector = (jnp.arange(kernels.shape[0], dtype=jnp.int32) == subpixel[0]).astype(f32)
    weights = dot("k,kt->t", selector, kernels)
    taps = kernels.shape[1]
    moved = sum(
        weights[t] * jnp.roll(folded, -(jitter[0] + t - taps // 2), axis=2) for t in range(taps)
    )
    spectrum = dot("nrx,gxf->gnrf", moved, jnp.asarray(fast_tables(length, groups, scan_rows)))
    upper, lower = spectrum[:, :, :height], spectrum[:, :, height:]
    spectrum = jnp.concatenate(
        [upper[..., :columns] + lower[..., columns:], lower[..., :columns] - upper[..., columns:]], 3
    )
    gathered = lax.all_to_all(spectrum, ("det", "sub"), split_axis=0, concat_axis=1, tiled=True)[0]
    visible = lax.all_gather(intersection[0], "row", axis=1, tiled=True).astype(f32)
    masked = dot("qb,brf->qrf", visible, gathered)
    cosine, sine = unit_circle(np.arange(scan_rows)[:, None] * np.arange(rows)[None, :], rows)
    me = lax.axis_index("row")
    cosine = jnp.asarray(cosine, f32)[:, me][:, None, None]
    sine = jnp.asarray(sine, f32)[:, me][:, None, None]
    real, imaginary = masked[..., :columns], masked[..., columns:]
    turned = jnp.concatenate([cosine * real + sine * imaginary, cosine * imaginary - sine * real], 2)
    slots = dot("ocq,qrf->ocrf", slot_table(owners[0, :, 0], rows, CAP), turned)
    return lax.psum_scatter(slots, "row", scatter_dimension=0, tiled=True)[None]


def split(value):
    high = value.astype(bf16)
    return high, (value - high.astype(f32)).astype(bf16)


def times(a, b):
    return jnp.dot(a, b, preferred_element_type=f32)


def scaled(factor, value):
    if abs(factor) < 1e-9:
        return None
    if abs(factor - 1.0) < 1e-9:
        return value
    return value * np.float32(factor)


def added(terms):
    terms = [term for term in terms if term is not None]
    return functools.reduce(lambda a, b: a + b, terms)


def fused_kernel(
    sizes, patterns, jitter, subpixel, kernels, intersection, owners, wigner, inner, turns,
    fast_high, fast_low, phases, out, kernels_here, intersection_here,
    owners_here, wigner_here, inner_here, phases_here, pixels, turn, table_high, table_low, outgoing,
    incoming, visible, slots, arrivals, small_sem, load_sem, send_sem, recv_sem, mask_send, mask_recv,
    slot_send, slot_recv,
):
    rows, dets, subs, scan_rows, height, columns, chunks, parts = sizes
    groups = dets * subs
    row = lax.axis_index("row")
    det = lax.axis_index("det")
    sub = lax.axis_index("sub")
    group = det * subs + sub
    pair = row // 2
    side = row - 2 * pair
    share = height // 2
    part = share // parts

    def wrapped(index, size):
        return jnp.where(index >= size, index - size, index)

    row_of = [row, 2 * pair + 1 - side, 2 * (1 - pair) + side, 2 * (1 - pair) + 1 - side]
    side_of = [side, 1 - side]
    det_of = [det] + [wrapped(det + k, dets) for k in range(1, dets)]
    sub_of = [sub] + [wrapped(sub + k, subs) for k in range(1, subs)]
    group_of = [d * subs + u for d in det_of for u in sub_of]
    group_order = list(range(groups))[::-1]
    near = [(m, dg) for dg in group_order for m in (1, 0) if (m, dg) != (0, 0)]
    peers = [(3, 0), (2, 0)] + near

    def row_at(offset):
        return row_of[offset]

    def group_at(offset):
        return group_of[offset]

    def device(dr, dg):
        return {"row": row_of[dr], "det": det_of[dg // subs], "sub": sub_of[dg % subs]}

    def rows_of(which, c):
        return pl.ds(pl.multiple_of(which * share + c * part, part), part)

    barrier = pltpu.get_barrier_semaphore()
    for dr, dg in peers:
        pl.semaphore_signal(
            barrier, inc=1, device_id=device(dr, dg), device_id_type=pl.DeviceIdType.MESH
        )

    chunk = pixels.shape[0] // chunks
    loads = [
        pltpu.make_async_copy(turns.at[group], turn, load_sem.at[0]),
        pltpu.make_async_copy(fast_high, table_high, load_sem.at[1]),
        pltpu.make_async_copy(fast_low, table_low, load_sem.at[2]),
    ]
    pieces = [
        pltpu.make_async_copy(
            patterns.at[0, pl.ds(k * chunk, chunk)], pixels.at[pl.ds(k * chunk, chunk)], load_sem.at[3 + k]
        )
        for k in range(chunks)
    ]
    small = [
        pltpu.make_async_copy(source, target, small_sem.at[k])
        for k, (source, target) in enumerate(
            [
                (wigner, wigner_here), (inner, inner_here), (kernels, kernels_here),
                (intersection, intersection_here), (owners, owners_here), (phases, phases_here),
            ]
        )
    ]
    for copy in small:
        copy.start()
    loads[0].start()
    for piece in pieces:
        piece.start()
    loads[1].start()
    loads[2].start()

    small[0].wait()
    small[1].wait()
    filter_real, filter_imaginary = wiener_parts(wigner_here[0], wigner_here[1])
    both = jnp.dot(
        jnp.concatenate([filter_real, filter_imaginary]), inner_here[...],
        precision=highest, preferred_element_type=f32,
    )
    lanes = inner_here.shape[1] // 2
    inner_real = both[:height, :lanes] + both[height:, lanes:]
    inner_imaginary = both[height:, :lanes] - both[:height, lanes:]
    loads[0].wait()
    matrix = []
    for k in range(pixels.shape[0] // lanes):
        cosine = turn[0, :, k * lanes : (k + 1) * lanes]
        sine = turn[1, :, k * lanes : (k + 1) * lanes]
        matrix.append(
            split(
                jnp.concatenate(
                    [inner_real * cosine + inner_imaginary * sine, inner_imaginary * cosine - inner_real * sine]
                )
            )
        )
    per_chunk = chunk // lanes
    folded = jnp.zeros((2 * height, pixels.shape[1]), f32)
    for k in range(chunks):
        mine = matrix[k * per_chunk : (k + 1) * per_chunk]
        high = jnp.concatenate([m[0] for m in mine], 1)
        low = jnp.concatenate([m[1] for m in mine], 1)
        pieces[k].wait()
        piece_high, piece_low = split(pixels[k * chunk : (k + 1) * chunk, :])
        folded = folded + (times(high, piece_high) + times(high, piece_low) + times(low, piece_high))
    folded_high, folded_low = split(folded)

    for copy in small[2:]:
        copy.wait()
    shifts = lax.broadcasted_iota(jnp.int32, (SHIFTS, columns), 0) - SHIFTS // 2
    taps = kernels.shape[0]
    weight = jnp.zeros((SHIFTS, columns), f32)
    for t in range(taps):
        weight = weight + jnp.where(
            shifts == jitter[0] + (t - taps // 2), kernels_here[t, subpixel[0]], 0.0
        )

    frequency = lax.broadcasted_iota(jnp.int32, visible.shape[1:], 0)
    tile = jnp.zeros(visible.shape[1:], f32)
    for q in range(scan_rows):
        tile = jnp.where(frequency == q, intersection_here[0, q].astype(f32), tile)
    visible[row] = tile

    pl.semaphore_wait(barrier, len(peers))
    masks = []
    for dr in range(1, rows):
        copy = pltpu.make_async_remote_copy(
            src_ref=visible.at[row], dst_ref=visible.at[row], send_sem=mask_send.at[dr],
            recv_sem=mask_recv.at[row], device_id=device(dr, 0), device_id_type=pl.DeviceIdType.MESH,
        )
        copy.start()
        masks.append(copy)

    loads[1].wait()
    loads[2].wait()
    sends = []

    def send(c, dg):
        for m in (1, 0):
            if (m, dg) == (0, 0):
                incoming[c, side, group] = outgoing[0, rows_of(side, c), :]
                continue
            copy = pltpu.make_async_remote_copy(
                src_ref=outgoing.at[dg, rows_of(side_of[m], c), :], dst_ref=incoming.at[c, side, group],
                send_sem=send_sem.at[c, m, dg], recv_sem=recv_sem.at[c, side, group],
                device_id=device(m, dg), device_id_type=pl.DeviceIdType.MESH,
            )
            copy.start()
            sends.append(copy)

    for dg in group_order:
        other = group_at(dg)
        high = table_high[other]
        product = times(folded_high, high) + times(folded_high, table_low[other]) + times(folded_low, high)
        real = product[:height, :columns] + product[height:, columns:]
        imaginary = product[height:, :columns] - product[:height, columns:]
        phase_real = jnp.sum(weight * phases_here[other, 0], axis=0, keepdims=True)
        phase_imaginary = jnp.sum(weight * phases_here[other, 1], axis=0, keepdims=True)
        outgoing[dg, :, :columns] = real * phase_real - imaginary * phase_imaginary
        outgoing[dg, :, columns:] = real * phase_imaginary + imaginary * phase_real
        send(0, dg)
    for c in range(1, parts):
        for dg in group_order:
            send(c, dg)

    owner = [owners_here[0, q] for q in range(scan_rows)]
    ranking = [
        sum([(owner[p] == owner[q]).astype(jnp.int32) for p in range(q)], jnp.int32(0))
        for q in range(scan_rows)
    ]
    sign = (1 - 2 * pair).astype(f32)
    chosen = {
        (m, k, q): jnp.where(
            (owner[q] == row_of[m]) & (ranking[q] == k), sign if q % 2 else jnp.float32(1.0), 0.0
        )
        for m in range(rows) for k in range(CAP) for q in range(scan_rows)
    }

    for m in range(1, rows):
        pltpu.make_async_remote_copy(
            src_ref=visible.at[row_at(m)], dst_ref=visible.at[row_at(m)], send_sem=mask_send.at[m],
            recv_sem=mask_recv.at[row_at(m)], device_id=device(m, 0), device_id_type=pl.DeviceIdType.MESH,
        ).wait_recv()

    slot_copies = []
    for c in range(parts):
        for m, dg in near:
            pltpu.make_async_remote_copy(
                src_ref=outgoing.at[dg, rows_of(side, c), :],
                dst_ref=incoming.at[c, side_of[m], group_at(dg)],
                send_sem=send_sem.at[c, m, dg], recv_sem=recv_sem.at[c, side_of[m], group_at(dg)],
                device_id=device(m, dg), device_id_type=pl.DeviceIdType.MESH,
            ).wait_recv()

        real = [None] * scan_rows
        imaginary = [None] * scan_rows
        for b in range(groups):
            values = [incoming[c, y, b] for y in range(2)]
            reals = [v[:, :columns] for v in values]
            imaginaries = [v[:, columns:] for v in values]
            for q in range(scan_rows):
                circle = [unit_circle(np.array(q * y), rows) for y in range(2)]
                keep = visible[b, q : q + 1, :]
                sum_real = added(
                    [scaled(c_, v) for (c_, _), v in zip(circle, reals)]
                    + [scaled(s_, v) for (_, s_), v in zip(circle, imaginaries)]
                )
                sum_imaginary = added(
                    [scaled(c_, v) for (c_, _), v in zip(circle, imaginaries)]
                    + [scaled(-s_, v) for (_, s_), v in zip(circle, reals)]
                )
                real[q] = added([real[q], keep * sum_real])
                imaginary[q] = added([imaginary[q], keep * sum_imaginary])

        for m in (3, 2, 1, 0):
            for k in range(CAP):
                slot_real = added([chosen[m, k, q] * real[q] for q in range(scan_rows)])
                slot_imaginary = added([chosen[m, k, q] * imaginary[q] for q in range(scan_rows)])
                if m == 0:
                    arrivals[c, row, k, :, :columns] = slot_real
                    arrivals[c, row, k, :, columns:] = slot_imaginary
                else:
                    slots[c, m, k, :, :columns] = slot_real
                    slots[c, m, k, :, columns:] = slot_imaginary
            if m:
                copy = pltpu.make_async_remote_copy(
                    src_ref=slots.at[c, m], dst_ref=arrivals.at[c, row],
                    send_sem=slot_send.at[c, m], recv_sem=slot_recv.at[c, row],
                    device_id=device(m, 0), device_id_type=pl.DeviceIdType.MESH,
                )
                copy.start()
                slot_copies.append(copy)

    for c in range(parts):
        for m in range(1, rows):
            pltpu.make_async_remote_copy(
                src_ref=slots.at[c, m], dst_ref=arrivals.at[c, row_at(m)],
                send_sem=slot_send.at[c, m], recv_sem=slot_recv.at[c, row_at(m)],
                device_id=device(m, 0), device_id_type=pl.DeviceIdType.MESH,
            ).wait_recv()
        for y in range(2):
            first = y * share + c * part
            out[0, 0, :, first : first + part, :] = arrivals[c, y] + arrivals[c, y + 2]
    for copy in masks + sends + slot_copies:
        copy.wait_send()


def fused(patterns, jitter, subpixel, kernels, intersection, owners, wigner):
    _, pixel_share, length = patterns.shape
    height, width = wigner.shape[1:]
    subs = lax.axis_size("sub")
    dets = lax.axis_size("det")
    groups = dets * subs
    rows = lax.axis_size("row")
    columns = length // groups
    scan_rows = owners.shape[1]
    chunks = 4
    parts = 2
    part = height // 2 // parts
    fast = fast_tables(length, groups, scan_rows)
    fast_high = fast.astype(bf16)
    fast_low = (fast - fast_high.astype(np.float32)).astype(bf16)
    vmem = pl.BlockSpec(memory_space=pltpu.VMEM)
    smem = pl.BlockSpec(memory_space=pltpu.SMEM)
    hbm = pl.BlockSpec(memory_space=pl.ANY)
    sizes = (rows, dets, subs, scan_rows, height, columns, chunks, parts)
    mask_rows = -(-scan_rows // 8) * 8
    dma = pltpu.SemaphoreType.DMA
    return pl.pallas_call(
        functools.partial(fused_kernel, sizes),
        out_shape=jax.ShapeDtypeStruct((1, 1, CAP, height, 2 * columns), f32),
        in_specs=[hbm, smem, smem] + [hbm] * 9,
        out_specs=vmem,
        scratch_shapes=[
            pltpu.SMEM(kernels.shape[::-1], f32),
            pltpu.SMEM((1, scan_rows), jnp.int32),
            pltpu.SMEM((1, scan_rows), jnp.int32),
            pltpu.VMEM(wigner.shape, f32),
            pltpu.VMEM((width, 256), f32),
            pltpu.VMEM((groups, 2, SHIFTS, columns), f32),
            pltpu.VMEM((pixel_share, length), f32),
            pltpu.VMEM((2, height, pixel_share), f32),
            pltpu.VMEM((groups, length, 2 * columns), bf16),
            pltpu.VMEM((groups, length, 2 * columns), bf16),
            pltpu.VMEM((groups, height, 2 * columns), f32),
            pltpu.VMEM((parts, 2, groups, part, 2 * columns), f32),
            pltpu.VMEM((rows, mask_rows, columns), f32),
            pltpu.VMEM((parts, rows, CAP, part, 2 * columns), f32),
            pltpu.VMEM((parts, rows, CAP, part, 2 * columns), f32),
            dma((6,)),
            dma((3 + chunks,)),
            dma((parts, 2, groups)),
            dma((parts, 2, groups)),
            dma((rows,)),
            dma((rows,)),
            dma((parts, rows)),
            dma((parts, rows)),
        ],
        compiler_params=pltpu.CompilerParams(
            collective_id=0, has_side_effects=True, vmem_limit_bytes=60 * 1024 * 1024
        ),
    )(
        patterns, jitter, subpixel, kernels.T, intersection.reshape(1, scan_rows),
        owners.reshape(1, scan_rows), wigner,
        jnp.asarray(inner_table(width, 128 // width)),
        jnp.asarray(row_tables(height, width, groups)),
        jnp.asarray(fast_high), jnp.asarray(fast_low),
        jnp.asarray(shift_tables(length, groups)),
    )


def per_device(patterns, jitter, subpixel, kernels, intersection, owners, wigner):
    _, pixel_share, length = patterns.shape
    height, width = wigner.shape[1:]
    groups = lax.axis_size(("det", "sub"))
    rows = lax.axis_size("row")
    one_block = groups == rows == owners.shape[1] == 4 and pixel_share % 1024 == 0
    tiles = height % 64 == 0 and (length // groups) % 128 == 0 and 128 % width == 0
    form = fused if one_block and tiles else general
    return form(patterns, jitter, subpixel, kernels, intersection, owners, wigner)


def solution(mesh):
    return jax.shard_map(
        per_device,
        mesh=mesh,
        in_specs=(
            P(("grp", "row"), ("det", "sub"), None),
            P(("grp", "row")),
            P(("grp", "row")),
            P(),
            P(("det", "sub"), None, "row"),
            P(("det", "sub"), None, None),
            P(),
        ),
        out_specs=P(("grp", "det", "sub"), "row", None, None, None),
        check_vma=False,
    )
```

```python
import functools
import math

import jax
import jax.numpy as jnp
import numpy as np
from jax import lax
from jax.experimental import pallas as pl
from jax.experimental.pallas import tpu as pltpu
from jax.sharding import PartitionSpec as P

CAP = 2
SHIFTS = 32

highest = lax.Precision.HIGHEST
f32 = jnp.float32
bf16 = jnp.bfloat16


def slot_table(column, owners_count, capacity):
    positions = jnp.arange(column.shape[0], dtype=jnp.int32)
    earlier = (column[:, None] == column[None, :]) & (positions[:, None] < positions[None, :])
    ranking = jnp.sum(earlier.astype(jnp.int32), axis=0)
    matches = (
        column[None, None, :] == jnp.arange(owners_count, dtype=jnp.int32)[:, None, None]
    ) & (ranking[None, None, :] == jnp.arange(capacity, dtype=jnp.int32)[None, :, None])
    return matches.astype(f32)


def unit_circle(products, length):
    angles = 2.0 * np.pi / length * np.mod(products, length)
    return np.cos(angles), np.sin(angles)


def fast_tables(length, groups, scan_rows):
    samples = np.arange(length)
    cosine, sine = unit_circle(samples[:, None] * samples[None, :], length)
    scale = 1.0 / math.sqrt(length * scan_rows)
    both = np.stack([cosine, sine]).reshape(2, length, groups, length // groups)
    return (both.transpose(2, 1, 0, 3) * scale).reshape(groups, length, -1).astype(np.float32)


def inner_table(width, repeats):
    index = np.arange(width)
    cosine, sine = unit_circle(index[:, None] * index[None, :], width)
    return np.concatenate([np.tile(cosine, repeats), np.tile(sine, repeats)], 1).astype(np.float32)


def row_tables(height, width, groups):
    pixels = np.arange(height * width)
    cosine, sine = unit_circle(np.arange(height)[:, None] * (pixels // width)[None, :], height)
    both = np.stack([cosine, sine]) / math.sqrt(height * width * width)
    return both.reshape(2, height, groups, -1).transpose(2, 0, 1, 3).astype(np.float32)


def shift_tables(length, groups):
    shifts = np.arange(SHIFTS) - SHIFTS // 2
    cosine, sine = unit_circle(shifts[:, None] * np.arange(length)[None, :], length)
    both = np.stack([cosine, sine]).reshape(2, SHIFTS, groups, length // groups)
    return both.transpose(2, 0, 1, 3).astype(np.float32)


def wiener_parts(real, imaginary):
    denominator = real * real + imaginary * imaginary + 0.1
    return real / denominator, -imaginary / denominator


def general(patterns, jitter, subpixel, kernels, intersection, owners, wigner):
    _, pixel_share, length = patterns.shape
    height, width = wigner.shape[1:]
    groups = lax.axis_size(("det", "sub"))
    rows = lax.axis_size("row")
    columns = length // groups
    block_pixels = pixel_share * groups // rows
    local_blocks = pixel_share // block_pixels
    scan_rows = owners.shape[1]
    group = lax.axis_index(("det", "sub"))
    dot = functools.partial(jnp.einsum, precision=highest)

    filter_real, filter_imaginary = wiener_parts(wigner[0], wigner[1])
    repeats = pixel_share // width
    table = jnp.asarray(inner_table(width, 1))
    cosine, sine = table[:, :width], table[:, width:]
    inner_real = dot("rx,xk->rk", filter_real, cosine) + dot("rx,xk->rk", filter_imaginary, sine)
    inner_imaginary = dot("rx,xk->rk", filter_imaginary, cosine) - dot("rx,xk->rk", filter_real, sine)
    inner_real, inner_imaginary = (jnp.tile(v, (1, repeats)) for v in (inner_real, inner_imaginary))
    turn = lax.dynamic_index_in_dim(jnp.asarray(row_tables(height, width, groups)), group, 0, False)
    matrix = jnp.concatenate(
        [inner_real * turn[0] + inner_imaginary * turn[1], inner_imaginary * turn[0] - inner_real * turn[1]]
    )
    folded = dot(
        "rnp,npx->nrx",
        matrix.reshape(2 * height, local_blocks, block_pixels),
        patterns[0].reshape(local_blocks, block_pixels, length),
    )
    selector = (jnp.arange(kernels.shape[0], dtype=jnp.int32) == subpixel[0]).astype(f32)
    weights = dot("k,kt->t", selector, kernels)
    taps = kernels.shape[1]
    moved = sum(
        weights[t] * jnp.roll(folded, -(jitter[0] + t - taps // 2), axis=2) for t in range(taps)
    )
    spectrum = dot("nrx,gxf->gnrf", moved, jnp.asarray(fast_tables(length, groups, scan_rows)))
    upper, lower = spectrum[:, :, :height], spectrum[:, :, height:]
    spectrum = jnp.concatenate(
        [upper[..., :columns] + lower[..., columns:], lower[..., :columns] - upper[..., columns:]], 3
    )
    gathered = lax.all_to_all(spectrum, ("det", "sub"), split_axis=0, concat_axis=1, tiled=True)[0]
    visible = lax.all_gather(intersection[0], "row", axis=1, tiled=True).astype(f32)
    masked = dot("qb,brf->qrf", visible, gathered)
    cosine, sine = unit_circle(np.arange(scan_rows)[:, None] * np.arange(rows)[None, :], rows)
    me = lax.axis_index("row")
    cosine = jnp.asarray(cosine, f32)[:, me][:, None, None]
    sine = jnp.asarray(sine, f32)[:, me][:, None, None]
    real, imaginary = masked[..., :columns], masked[..., columns:]
    turned = jnp.concatenate([cosine * real + sine * imaginary, cosine * imaginary - sine * real], 2)
    slots = dot("ocq,qrf->ocrf", slot_table(owners[0, :, 0], rows, CAP), turned)
    return lax.psum_scatter(slots, "row", scatter_dimension=0, tiled=True)[None]


def split(value):
    high = value.astype(bf16)
    return high, (value - high.astype(f32)).astype(bf16)


def times(a, b):
    return jnp.dot(a, b, preferred_element_type=f32)


def scaled(factor, value):
    if abs(factor) < 1e-9:
        return None
    if abs(factor - 1.0) < 1e-9:
        return value
    return value * np.float32(factor)


def added(terms):
    terms = [term for term in terms if term is not None]
    return functools.reduce(lambda a, b: a + b, terms)


def fused_kernel(
    sizes, patterns, jitter, subpixel, kernels, intersection, owners, wigner, inner, turns,
    fast_high, fast_low, phases, out, kernels_here, intersection_here,
    owners_here, wigner_here, inner_here, phases_here, pixels, turn, table_high, table_low, outgoing,
    incoming, visible, slots, arrivals, small_sem, load_sem, send_sem, recv_sem, mask_send, mask_recv,
    slot_send, slot_recv,
):
    rows, dets, subs, scan_rows, height, columns, chunks, parts = sizes
    groups = dets * subs
    row = lax.axis_index("row")
    det = lax.axis_index("det")
    sub = lax.axis_index("sub")
    group = det * subs + sub
    pair = row // 2
    side = row - 2 * pair
    share = height // 2
    part = share // parts

    def wrapped(index, size):
        return jnp.where(index >= size, index - size, index)

    row_of = [row, 2 * pair + 1 - side, 2 * (1 - pair) + side, 2 * (1 - pair) + 1 - side]
    side_of = [side, 1 - side]
    det_of = [det] + [wrapped(det + k, dets) for k in range(1, dets)]
    sub_of = [sub] + [wrapped(sub + k, subs) for k in range(1, subs)]
    group_of = [d * subs + u for d in det_of for u in sub_of]
    group_order = list(range(groups))[::-1]
    near = [(m, dg) for dg in group_order for m in (1, 0) if (m, dg) != (0, 0)]
    peers = [(3, 0), (2, 0)] + near

    def row_at(offset):
        return row_of[offset]

    def group_at(offset):
        return group_of[offset]

    def device(dr, dg):
        return {"row": row_of[dr], "det": det_of[dg // subs], "sub": sub_of[dg % subs]}

    def rows_of(which, c):
        return pl.ds(pl.multiple_of(which * share + c * part, part), part)

    barrier = pltpu.get_barrier_semaphore()
    for dr, dg in peers:
        pl.semaphore_signal(
            barrier, inc=1, device_id=device(dr, dg), device_id_type=pl.DeviceIdType.MESH
        )

    chunk = pixels.shape[0] // chunks
    loads = [
        pltpu.make_async_copy(turns.at[group], turn, load_sem.at[0]),
        pltpu.make_async_copy(fast_high, table_high, load_sem.at[1]),
        pltpu.make_async_copy(fast_low, table_low, load_sem.at[2]),
    ]
    pieces = [
        pltpu.make_async_copy(
            patterns.at[0, pl.ds(k * chunk, chunk)], pixels.at[pl.ds(k * chunk, chunk)], load_sem.at[3 + k]
        )
        for k in range(chunks)
    ]
    small = [
        pltpu.make_async_copy(source, target, small_sem.at[k])
        for k, (source, target) in enumerate(
            [
                (wigner, wigner_here), (inner, inner_here), (kernels, kernels_here),
                (intersection, intersection_here), (owners, owners_here), (phases, phases_here),
            ]
        )
    ]
    for copy in small:
        copy.start()
    loads[0].start()
    for piece in pieces:
        piece.start()
    loads[1].start()
    loads[2].start()

    small[0].wait()
    small[1].wait()
    filter_real, filter_imaginary = wiener_parts(wigner_here[0], wigner_here[1])
    both = jnp.dot(
        jnp.concatenate([filter_real, filter_imaginary]), inner_here[...],
        precision=highest, preferred_element_type=f32,
    )
    lanes = inner_here.shape[1] // 2
    inner_real = both[:height, :lanes] + both[height:, lanes:]
    inner_imaginary = both[height:, :lanes] - both[:height, lanes:]
    loads[0].wait()
    matrix = []
    for k in range(pixels.shape[0] // lanes):
        cosine = turn[0, :, k * lanes : (k + 1) * lanes]
        sine = turn[1, :, k * lanes : (k + 1) * lanes]
        matrix.append(
            split(
                jnp.concatenate(
                    [inner_real * cosine + inner_imaginary * sine, inner_imaginary * cosine - inner_real * sine]
                )
            )
        )
    per_chunk = chunk // lanes
    folded = jnp.zeros((2 * height, pixels.shape[1]), f32)
    for k in range(chunks):
        mine = matrix[k * per_chunk : (k + 1) * per_chunk]
        high = jnp.concatenate([m[0] for m in mine], 1)
        low = jnp.concatenate([m[1] for m in mine], 1)
        pieces[k].wait()
        piece_high, piece_low = split(pixels[k * chunk : (k + 1) * chunk, :])
        folded = folded + (times(high, piece_high) + times(high, piece_low) + times(low, piece_high))
    folded_high, folded_low = split(folded)

    for copy in small[2:]:
        copy.wait()
    shifts = lax.broadcasted_iota(jnp.int32, (SHIFTS, columns), 0) - SHIFTS // 2
    taps = kernels.shape[0]
    weight = jnp.zeros((SHIFTS, columns), f32)
    for t in range(taps):
        weight = weight + jnp.where(
            shifts == jitter[0] + (t - taps // 2), kernels_here[t, subpixel[0]], 0.0
        )

    frequency = lax.broadcasted_iota(jnp.int32, visible.shape[1:], 0)
    tile = jnp.zeros(visible.shape[1:], f32)
    for q in range(scan_rows):
        tile = jnp.where(frequency == q, intersection_here[0, q].astype(f32), tile)
    visible[row] = tile

    pl.semaphore_wait(barrier, len(peers))
    masks = []
    for dr in range(1, rows):
        copy = pltpu.make_async_remote_copy(
            src_ref=visible.at[row], dst_ref=visible.at[row], send_sem=mask_send.at[dr],
            recv_sem=mask_recv.at[row], device_id=device(dr, 0), device_id_type=pl.DeviceIdType.MESH,
        )
        copy.start()
        masks.append(copy)

    loads[1].wait()
    loads[2].wait()
    sends = []

    def send(c, dg):
        for m in (1, 0):
            if (m, dg) == (0, 0):
                incoming[c, side, group] = outgoing[0, rows_of(side, c), :]
                continue
            copy = pltpu.make_async_remote_copy(
                src_ref=outgoing.at[dg, rows_of(side_of[m], c), :], dst_ref=incoming.at[c, side, group],
                send_sem=send_sem.at[c, m, dg], recv_sem=recv_sem.at[c, side, group],
                device_id=device(m, dg), device_id_type=pl.DeviceIdType.MESH,
            )
            copy.start()
            sends.append(copy)

    for dg in group_order:
        other = group_at(dg)
        high = table_high[other]
        product = times(folded_high, high) + times(folded_high, table_low[other]) + times(folded_low, high)
        real = product[:height, :columns] + product[height:, columns:]
        imaginary = product[height:, :columns] - product[:height, columns:]
        phase_real = jnp.sum(weight * phases_here[other, 0], axis=0, keepdims=True)
        phase_imaginary = jnp.sum(weight * phases_here[other, 1], axis=0, keepdims=True)
        outgoing[dg, :, :columns] = real * phase_real - imaginary * phase_imaginary
        outgoing[dg, :, columns:] = real * phase_imaginary + imaginary * phase_real
        send(0, dg)
    for c in range(1, parts):
        for dg in group_order:
            send(c, dg)

    owner = [owners_here[0, q] for q in range(scan_rows)]
    ranking = [
        sum([(owner[p] == owner[q]).astype(jnp.int32) for p in range(q)], jnp.int32(0))
        for q in range(scan_rows)
    ]
    sign = (1 - 2 * pair).astype(f32)
    chosen = {
        (m, k, q): jnp.where(
            (owner[q] == row_of[m]) & (ranking[q] == k), sign if q % 2 else jnp.float32(1.0), 0.0
        )
        for m in range(rows) for k in range(CAP) for q in range(scan_rows)
    }

    for m in range(1, rows):
        pltpu.make_async_remote_copy(
            src_ref=visible.at[row_at(m)], dst_ref=visible.at[row_at(m)], send_sem=mask_send.at[m],
            recv_sem=mask_recv.at[row_at(m)], device_id=device(m, 0), device_id_type=pl.DeviceIdType.MESH,
        ).wait_recv()

    slot_copies = []
    for c in range(parts):
        for m, dg in near:
            pltpu.make_async_remote_copy(
                src_ref=outgoing.at[dg, rows_of(side, c), :],
                dst_ref=incoming.at[c, side_of[m], group_at(dg)],
                send_sem=send_sem.at[c, m, dg], recv_sem=recv_sem.at[c, side_of[m], group_at(dg)],
                device_id=device(m, dg), device_id_type=pl.DeviceIdType.MESH,
            ).wait_recv()

        real = [None] * scan_rows
        imaginary = [None] * scan_rows
        for b in range(groups):
            values = [incoming[c, y, b] for y in range(2)]
            reals = [v[:, :columns] for v in values]
            imaginaries = [v[:, columns:] for v in values]
            for q in range(scan_rows):
                circle = [unit_circle(np.array(q * y), rows) for y in range(2)]
                keep = visible[b, q : q + 1, :]
                sum_real = added(
                    [scaled(c_, v) for (c_, _), v in zip(circle, reals)]
                    + [scaled(s_, v) for (_, s_), v in zip(circle, imaginaries)]
                )
                sum_imaginary = added(
                    [scaled(c_, v) for (c_, _), v in zip(circle, imaginaries)]
                    + [scaled(-s_, v) for (_, s_), v in zip(circle, reals)]
                )
                real[q] = added([real[q], keep * sum_real])
                imaginary[q] = added([imaginary[q], keep * sum_imaginary])

        for m in (3, 2, 1, 0):
            for k in range(CAP):
                slot_real = added([chosen[m, k, q] * real[q] for q in range(scan_rows)])
                slot_imaginary = added([chosen[m, k, q] * imaginary[q] for q in range(scan_rows)])
                if m == 0:
                    arrivals[c, row, k, :, :columns] = slot_real
                    arrivals[c, row, k, :, columns:] = slot_imaginary
                else:
                    slots[c, m, k, :, :columns] = slot_real
                    slots[c, m, k, :, columns:] = slot_imaginary
            if m:
                copy = pltpu.make_async_remote_copy(
                    src_ref=slots.at[c, m], dst_ref=arrivals.at[c, row],
                    send_sem=slot_send.at[c, m], recv_sem=slot_recv.at[c, row],
                    device_id=device(m, 0), device_id_type=pl.DeviceIdType.MESH,
                )
                copy.start()
                slot_copies.append(copy)

    for c in range(parts):
        for m in range(1, rows):
            pltpu.make_async_remote_copy(
                src_ref=slots.at[c, m], dst_ref=arrivals.at[c, row_at(m)],
                send_sem=slot_send.at[c, m], recv_sem=slot_recv.at[c, row_at(m)],
                device_id=device(m, 0), device_id_type=pl.DeviceIdType.MESH,
            ).wait_recv()
        for y in range(2):
            first = y * share + c * part
            for h in range(2):
                out[h, :, first : first + part, :] = arrivals[c, y + 2 * h]
    for copy in masks + sends + slot_copies:
        copy.wait_send()


def fused(patterns, jitter, subpixel, kernels, intersection, owners, wigner):
    _, pixel_share, length = patterns.shape
    height, width = wigner.shape[1:]
    subs = lax.axis_size("sub")
    dets = lax.axis_size("det")
    groups = dets * subs
    rows = lax.axis_size("row")
    columns = length // groups
    scan_rows = owners.shape[1]
    chunks = 4
    parts = 2
    part = height // 2 // parts
    fast = fast_tables(length, groups, scan_rows)
    fast_high = fast.astype(bf16)
    fast_low = (fast - fast_high.astype(np.float32)).astype(bf16)
    vmem = pl.BlockSpec(memory_space=pltpu.VMEM)
    smem = pl.BlockSpec(memory_space=pltpu.SMEM)
    hbm = pl.BlockSpec(memory_space=pl.ANY)
    sizes = (rows, dets, subs, scan_rows, height, columns, chunks, parts)
    mask_rows = -(-scan_rows // 8) * 8
    dma = pltpu.SemaphoreType.DMA
    halves = pl.pallas_call(
        functools.partial(fused_kernel, sizes),
        out_shape=jax.ShapeDtypeStruct((2, CAP, height, 2 * columns), f32),
        in_specs=[hbm, smem, smem] + [hbm] * 9,
        out_specs=vmem,
        scratch_shapes=[
            pltpu.SMEM(kernels.shape[::-1], f32),
            pltpu.SMEM((1, scan_rows), jnp.int32),
            pltpu.SMEM((1, scan_rows), jnp.int32),
            pltpu.VMEM(wigner.shape, f32),
            pltpu.VMEM((width, 256), f32),
            pltpu.VMEM((groups, 2, SHIFTS, columns), f32),
            pltpu.VMEM((pixel_share, length), f32),
            pltpu.VMEM((2, height, pixel_share), f32),
            pltpu.VMEM((groups, length, 2 * columns), bf16),
            pltpu.VMEM((groups, length, 2 * columns), bf16),
            pltpu.VMEM((groups, height, 2 * columns), f32),
            pltpu.VMEM((parts, 2, groups, part, 2 * columns), f32),
            pltpu.VMEM((rows, mask_rows, columns), f32),
            pltpu.VMEM((parts, rows, CAP, part, 2 * columns), f32),
            pltpu.VMEM((parts, rows, CAP, part, 2 * columns), f32),
            dma((6,)),
            dma((3 + chunks,)),
            dma((parts, 2, groups)),
            dma((parts, 2, groups)),
            dma((rows,)),
            dma((rows,)),
            dma((parts, rows)),
            dma((parts, rows)),
        ],
        compiler_params=pltpu.CompilerParams(
            collective_id=0, has_side_effects=True, vmem_limit_bytes=60 * 1024 * 1024
        ),
    )(
        patterns, jitter, subpixel, kernels.T, intersection.reshape(1, scan_rows),
        owners.reshape(1, scan_rows), wigner,
        jnp.asarray(inner_table(width, 128 // width)),
        jnp.asarray(row_tables(height, width, groups)),
        jnp.asarray(fast_high), jnp.asarray(fast_low),
        jnp.asarray(shift_tables(length, groups)),
    )
    return (halves[0] + halves[1])[None, None]


def per_device(patterns, jitter, subpixel, kernels, intersection, owners, wigner):
    _, pixel_share, length = patterns.shape
    height, width = wigner.shape[1:]
    groups = lax.axis_size(("det", "sub"))
    rows = lax.axis_size("row")
    one_block = groups == rows == owners.shape[1] == 4 and pixel_share % 1024 == 0
    tiles = height % 64 == 0 and (length // groups) % 128 == 0 and 128 % width == 0
    form = fused if one_block and tiles else general
    return form(patterns, jitter, subpixel, kernels, intersection, owners, wigner)


def solution(mesh):
    return jax.shard_map(
        per_device,
        mesh=mesh,
        in_specs=(
            P(("grp", "row"), ("det", "sub"), None),
            P(("grp", "row")),
            P(("grp", "row")),
            P(),
            P(("det", "sub"), None, "row"),
            P(("det", "sub"), None, None),
            P(),
        ),
        out_specs=P(("grp", "det", "sub"), "row", None, None, None),
        check_vma=False,
    )
```
